768 devices in a mesh: comp: 2 (over z_hi), col: 384 (over x, y, z_lo, core).
Axes of the slice: x: 4, y: 8, z: 12 (z_hi: 2, z_lo: 6; z = z_hi * 6 + z_lo), core: 2. Of those that a mesh axis runs over, the one named last changes fastest.
Arguments:
- column_state: float32 [2, 2, 80, 786432], P('comp', None, None, 'col'), may hold values from -6 to 6
- neighbour_offsets: int32 [2, 6, 786432], P('comp', None, 'col'), may hold values from -256 to 256
- edge_coefficients: float32 [2, 6, 786432], P('comp', None, 'col'), may hold values from 0.02 to 0.15
- active_levels: int32 [2, 786432], P('comp', 'col'), may hold values from 0 to 80, as said below
- intersection_offsets: int32 [2, 8, 786432], P('comp', None, 'col'), may hold values from -256 to 256, as said below
- intersection_weights: float32 [2, 8, 786432], P('comp', None, 'col'), may hold values from 0 to 1, as said below
- relaxation: float32 [2, 2], P('comp'), may hold values from 0.2 to 0.6
Outputs:
- coupled_state: float32 [2, 2, 80, 786432], P('comp', None, None, 'col')
- remapped: float32 [2, 2, 786432], P('comp', None, 'col')
The draws below stay inside these ranges and needn't reach their ends.
Inputs may be any that keep to these rules, and one draw needn't show every extreme that they name: `active_levels`: atmosphere columns have 72 active levels; ocean columns 0 on land, else 8 or more. `intersection_offsets`: each intersection source lies within 256 columns of the destination's position in the other component's order. `intersection_weights`: each destination column has 1 to 8 used intersection slots, the first ones; unused slots have weight 0.
All inputs are finite; a program needn't handle non-finite values.
Results may differ from the reference program's by a relative error of at most 0.00008.
Values sent between devices are 32-bit elements; how exact they have to be, the bound alone decides.
No kernel may reach another device: no remote copies, remote signals or barrier semaphores. Data moves between devices by JAX's collectives and lax.ppermute only.
A program may use at most 32 MiB of HBM per device.

```python
import math
import jax
import jax.numpy as jnp

NF = 2
LEV = 80
ATM_LEV = 72
KN = 6
KR = 8
COL_DEV = 2048
HALO = 256
NCOL = 786432


def edge_offsets(key, lists_n):
    columns = jnp.arange(NCOL, dtype=jnp.int32)
    offsets = jax.random.randint(key, (2, lists_n, NCOL), -HALO, HALO + 1, dtype=jnp.int32)
    position = columns % COL_DEV
    lowest = jnp.where(position == 0, -HALO, offsets[:, 0, :])
    leading = jnp.where(position == COL_DEV - 1, HALO, lowest)
    return offsets.at[:, 0, :].set(leading).astype(jnp.int32)


def draw_neighbour_offsets(key, part):
    key = jax.random.fold_in(key, 11)
    return edge_offsets(key, KN)


def draw_intersection_offsets(key, part):
    key = jax.random.fold_in(key, 23)
    return edge_offsets(key, KR)


def draw_active_levels(key, part):
    key = jax.random.fold_in(key, 37)
    land_key, depth_key = jax.random.split(key)
    is_land = jax.random.randint(land_key, (NCOL,), 0, 10, dtype=jnp.int32) < 3
    depths = jax.random.randint(depth_key, (NCOL,), 8, LEV + 1, dtype=jnp.int32)
    ocean_levels = jnp.where(is_land, 0, depths)
    ocean_levels = ocean_levels.at[0].set(LEV)
    air_levels = jnp.full((NCOL,), ATM_LEV, jnp.int32)
    return jnp.stack([air_levels, ocean_levels]).astype(jnp.int32)


def draw_intersection_weights(key, part):
    key = jax.random.fold_in(key, 41)
    count_key, value_key = jax.random.split(key)
    used = jax.random.randint(count_key, (2, 1, NCOL), 1, KR + 1, dtype=jnp.int32)
    used = used.at[:, :, 0].set(KR)
    slots = jnp.arange(KR, dtype=jnp.int32)[None, :, None]
    values = jnp.exp(jax.random.uniform(value_key, (2, KR, NCOL), jnp.float32, math.log(0.05), math.log(0.4)))
    return jnp.where(slots < used, values, 0.0).astype(jnp.float32)


def level_of(stream_key, extent, shards, low, top_value):
    level = 1.0
    for axis_at, blocks in shards:
        steps = jax.random.uniform(jax.random.fold_in(jax.random.fold_in(stream_key, 6), axis_at), (blocks,), jnp.float32, low / len(shards), top_value / len(shards))
        level = level * jnp.repeat(jnp.exp(steps), extent[axis_at] // blocks).reshape((-1,) + (1,) * (len(extent) - 1 - axis_at))
    return level


def noise(rng, extent, width, limit, cuts=(), kind=jnp.bfloat16):
    result = jax.random.normal(rng, extent, jnp.float32) * width
    if len(cuts) > 0:
        result = level_of(rng, extent, cuts, -0.22, 0.18) * result
    return jnp.clip(result, min=-limit, max=limit).astype(kind)


def setup_inputs(seed: int = 0) -> dict:
    key_list = jax.random.split(jax.random.key(seed), 8)
    column_state = noise(key_list[0], (2, NF, LEV, NCOL), 1.0, 6.0, ((0, 2), (3, 384)), jnp.float32)
    neighbour_offsets = draw_neighbour_offsets(jax.random.fold_in(key_list[7], 71), 0)
    edge_coefficients = jnp.clip(jnp.exp(math.log(0.15) - 2.014903 * jax.random.uniform(key_list[2], (2, KN, NCOL), jnp.float32) ** level_of(key_list[2], (2, KN, NCOL), ((0, 2), (2, 384)), -0.2, 0.2)), 0.02, 0.15)
    active_levels = draw_active_levels(jax.random.fold_in(key_list[7], 71), 0)
    intersection_offsets = draw_intersection_offsets(jax.random.fold_in(key_list[7], 71), 0)
    intersection_weights = draw_intersection_weights(jax.random.fold_in(key_list[7], 71), 0)
    relaxation = jnp.clip(0.2 + 0.400000021 * jax.random.uniform(key_list[6], (2, NF), jnp.float32) ** level_of(key_list[6], (2, NF), ((0, 2),), -0.2, 0.2), 0.2, 0.6)
    return {"column_state": column_state, "neighbour_offsets": neighbour_offsets, "edge_coefficients": edge_coefficients, "active_levels": active_levels, "intersection_offsets": intersection_offsets, "intersection_weights": intersection_weights, "relaxation": relaxation}


def widen_columns(values):
    padding = [(0, 0)] * (values.ndim - 1) + [(HALO, HALO)]
    return jnp.pad(values, padding)


def relax_columns(fields, neighbour_offsets, edge_coefficients, active_levels):
    padded = widen_columns(fields)
    position = jnp.arange(NCOL, dtype=jnp.int32) + HALO
    levels = jnp.arange(LEV, dtype=jnp.int32)[:, None]
    results = []
    for group in range(2):
        centre = fields[group]
        summed = jnp.zeros_like(centre)
        for entry in range(KN):
            nearby = jnp.take(padded[group], position + neighbour_offsets[group, entry], axis=2)
            summed = summed + edge_coefficients[group, entry][None, None, :] * (nearby - centre)
        wet_mask = (levels < active_levels[group][None, :]).astype(jnp.float32)
        results.append(centre + wet_mask * summed)
    return jnp.stack(results)


def reference(column_state, neighbour_offsets, edge_coefficients, active_levels, intersection_offsets, intersection_weights, relaxation):
    advanced = relax_columns(column_state, neighbour_offsets, edge_coefficients, active_levels)
    advanced = relax_columns(advanced, neighbour_offsets, edge_coefficients, active_levels)
    surface = column_state[:, :, 0, :]
    padded = widen_columns(surface[::-1])
    position = jnp.arange(NCOL, dtype=jnp.int32) + HALO
    results = []
    for group in range(2):
        summed = jnp.zeros((NF, NCOL), jnp.float32)
        for entry in range(KR):
            nearby = jnp.take(padded[group], position + intersection_offsets[group, entry], axis=1)
            summed = summed + intersection_weights[group, entry][None, :] * nearby
        results.append(summed)
    remapped = jnp.stack(results)
    levels = jnp.arange(LEV, dtype=jnp.int32)[:, None]
    surface_mask = ((levels == 0) & (levels < active_levels[:, None, None, :])).astype(jnp.float32)
    coupled_state = advanced + surface_mask * (relaxation[:, :, None, None] * (remapped[:, :, None, :] - advanced))
    return coupled_state, remapped
```

```python
import functools

import jax
import jax.numpy as jnp
from jax import lax
from jax.experimental import pallas as pl
from jax.experimental.pallas import tpu as pltpu
from jax.sharding import PartitionSpec as P

NF = 2
LEV = 80
ROWS = NF * LEV
COLS = 2048
HALO = 256
EDGE = 2 * HALO
KN = 6
KR = 8
BLOCK = 256
WINDOW = BLOCK + 2 * HALO
MID = COLS + 2 * HALO
SENT = ROWS + 8
LANES = 128
PANEL = 16
PACK_MIB = 60
RUN = 12

ANY = pl.BlockSpec(memory_space=pl.ANY)
HBM = pl.BlockSpec(memory_space=pltpu.HBM)
VMEM = pl.BlockSpec(memory_space=pltpu.VMEM)


def params(mib):
    return pltpu.CompilerParams(vmem_limit_bytes=mib << 20)


def on_first_core():
    return lax.rem(lax.axis_index("col"), 2) == 0


def pack_kernel(state, off_in, coef_in, act_in, beside, chip, surf, tiles, off, coef, act, sems):
    first = on_first_core()
    lists = [
        pltpu.make_async_copy(source, target, sems.at[4 + at])
        for at, (source, target) in enumerate(((off_in, off), (coef_in, coef), (act_in, act)))
    ]
    rows = [
        pltpu.make_async_copy(state.at[pl.ds(LEV * field, 8), :], tiles.at[field], sems.at[2 + field])
        for field in range(NF)
    ]

    def send(out, high, at):
        start = COLS - EDGE if high else 0
        copy = pltpu.make_async_copy(state.at[:, pl.ds(start, EDGE)], out.at[pl.ds(0, ROWS), :], sems.at[at])
        copy.start()
        return copy

    def fill(out, high):
        out[ROWS + KN : SENT, :] = jnp.zeros((8 - KN, EDGE), jnp.float32)
        for part in range(HALO // LANES):
            j = (COLS - HALO if high else 0) // LANES + part
            here = slice(part * LANES, (part + 1) * LANES)
            there = slice(HALO + part * LANES, HALO + (part + 1) * LANES)
            for k in range(KN):
                out[ROWS + k : ROWS + k + 1, here] = off[k, j : j + 1, :].astype(jnp.float32)
                out[ROWS + k : ROWS + k + 1, there] = coef[k, j : j + 1, :]
            out[ROWS + KN : ROWS + KN + 1, here] = act[:, j * LANES : (j + 1) * LANES].astype(jnp.float32)

    def both(high):
        copies = [send(beside, high, 0), send(chip, not high, 1)] + rows
        for copy in lists + rows:
            copy.start()
        for copy in lists:
            copy.wait()
        fill(beside, high)
        fill(chip, not high)
        for copy in copies:
            copy.wait()

    @pl.when(first)
    def _():
        both(False)

    @pl.when(jnp.logical_not(first))
    def _():
        both(True)

    for field in range(NF):
        surf[field : field + 1, :] = tiles[field, 0:1, :]


def pack(state, off, coef, act):
    sent = jax.ShapeDtypeStruct((SENT, EDGE), jnp.float32)
    return pl.pallas_call(
        pack_kernel,
        out_shape=(sent, sent, jax.ShapeDtypeStruct((NF, COLS), jnp.float32)),
        in_specs=[HBM, HBM, HBM, HBM],
        out_specs=(VMEM, VMEM, VMEM),
        scratch_shapes=[
            pltpu.VMEM((NF, 8, COLS), jnp.float32),
            pltpu.VMEM(off.shape, off.dtype),
            pltpu.VMEM(coef.shape, coef.dtype),
            pltpu.VMEM(act.shape, act.dtype),
            pltpu.SemaphoreType.DMA((7,)),
        ],
        compiler_params=params(PACK_MIB),
        name="pack",
    )(state, off, coef, act)


def from_far():
    place = lax.rem(lax.axis_index("col"), RUN)
    return jnp.logical_or(place == 0, place == RUN - 1)


def widen_kernel(chip, near, far, surf, out, tiles, sems):
    first = on_first_core()

    def bring(source, left, at):
        start = HALO if left else 0
        copies = [
            pltpu.make_async_copy(
                source.at[pl.ds(LEV * field, 8), pl.ds(start, HALO)],
                tiles.at[0 if left else 1, field],
                sems.at[NF * at + field],
            )
            for field in range(NF)
        ]
        for copy in copies:
            copy.start()
        return copies

    def both(source, left):
        for copy in bring(source, left, 0) + bring(chip, not left, 1):
            copy.wait()

    for source, is_far in ((far, True), (near, False)):
        for left in (True, False):

            @pl.when(jnp.logical_and(from_far() == is_far, first == left))
            def _(source=source, left=left):
                both(source, left)

    out[:, HALO : HALO + COLS] = surf[...]
    for field in range(NF):
        out[field : field + 1, 0:HALO] = tiles[0, field, 0:1, :]
        out[field : field + 1, HALO + COLS :] = tiles[1, field, 0:1, :]


def widen(chip, near, far, surf):
    return pl.pallas_call(
        widen_kernel,
        out_shape=jax.ShapeDtypeStruct((NF, MID), jnp.float32),
        in_specs=[ANY, ANY, ANY, VMEM],
        out_specs=VMEM,
        scratch_shapes=[pltpu.VMEM((2, NF, 8, HALO), jnp.float32), pltpu.SemaphoreType.DMA((2 * NF,))],
        compiler_params=params(2),
        name="widen",
    )(chip, near, far, surf)


def build_table(table, off, coef, first_panel):
    for part in range(BLOCK // LANES):
        at = pl.ds(first_panel + part, 1)
        lane = lax.broadcasted_iota(jnp.int32, (PANEL, LANES), 1)
        row = lax.broadcasted_iota(jnp.int32, (PANEL, LANES), 0)
        shift = lane - row + (HALO + part * LANES)
        offs = [jnp.broadcast_to(off[k, at, :], (PANEL, LANES)) for k in range(KN)]
        coefs = [jnp.broadcast_to(coef[k, at, :], (PANEL, LANES)) for k in range(KN)]
        high, low = [], []
        for k in range(KN):
            merged = coefs[k]
            for j in range(KN):
                if j != k:
                    merged = merged + jnp.where(offs[j] == offs[k], coefs[j], 0.0)
            top = merged.astype(jnp.bfloat16)
            high.append(top)
            low.append((merged - top.astype(jnp.float32)).astype(jnp.bfloat16))
        place = [(o + shift).astype(jnp.int16) for o in offs]
        none = jnp.zeros((PANEL, LANES), jnp.bfloat16)
        for start in range(0, WINDOW, PANEL):
            if start + PANEL <= part * LANES or start >= part * LANES + LANES + 2 * HALO:
                first, second = none, none
            else:
                first, second = none, none
                for k in range(KN):
                    hit = place[k] == jnp.int16(start)
                    first = jnp.where(hit, high[k], first)
                    second = jnp.where(hit, low[k], second)
            rows = slice(start, start + PANEL)
            table[rows, part * LANES : (part + 1) * LANES] = first
            table[rows, BLOCK + part * LANES : BLOCK + (part + 1) * LANES] = second


def split_into(parts, cols, value):
    top = value.astype(jnp.bfloat16)
    parts[0:ROWS, cols] = top
    parts[ROWS : 2 * ROWS, cols] = (value - top.astype(jnp.float32)).astype(jnp.bfloat16)


def relaxed(parts, table, start, centre, total, act):
    window = slice(start, start + WINDOW)
    both = jnp.dot(parts[:, window], table[:, 0:BLOCK], preferred_element_type=jnp.float32)
    rest = jnp.dot(parts[0:ROWS, window], table[:, BLOCK:], preferred_element_type=jnp.float32)
    gathered = both[0:ROWS] + both[ROWS:] + rest
    row = lax.broadcasted_iota(jnp.int32, (ROWS, BLOCK), 0)
    level = jnp.where(row >= LEV, row - LEV, row)
    return centre + jnp.where(level < act, gathered - total * centre, 0.0)


INSIDE = COLS - 2 * HALO
OWN = COLS // BLOCK


def totals_of(totals, coef, start, count):
    for j in range(count):
        total = coef[0, j : j + 1, :]
        for k in range(1, KN):
            total = total + coef[k, j : j + 1, :]
        totals[:, start + j * LANES : start + (j + 1) * LANES] = total


def inside_kernel(state, off, coef, act, tables, mid, parts2, out, parts, totals, done, sems):
    def table_of(b, carry):
        build_table(tables.at[b], off, coef, b * (BLOCK // LANES))
        return carry

    lax.fori_loop(0, OWN, table_of, 0)
    totals_of(totals, coef, 0, COLS // LANES)
    for b in range(OWN):
        cols = slice(b * BLOCK, (b + 1) * BLOCK)
        split_into(parts, cols, state[:, cols])
    for b in range(1, OWN - 1):
        cols = slice(b * BLOCK, (b + 1) * BLOCK)
        value = relaxed(parts, tables.at[b], (b - 1) * BLOCK, state[:, cols], totals[:, cols], act[:, cols])
        there = slice((b - 1) * BLOCK, b * BLOCK)
        mid[:, there] = value
        split_into(parts2, there, value)
    copies = []
    for b in range(2, OWN - 2):
        cols = slice(b * BLOCK, (b + 1) * BLOCK)
        centre = mid[:, (b - 1) * BLOCK : b * BLOCK]
        here = slice((b - 2) * BLOCK, (b - 1) * BLOCK)
        done[:, here] = relaxed(parts2, tables.at[b], (b - 2) * BLOCK, centre, totals[:, cols], act[:, cols])
        copy = pltpu.make_async_copy(
            done.at[:, pl.ds((b - 2) * BLOCK, BLOCK)], out.at[:, pl.ds(b * BLOCK, BLOCK)], sems.at[b - 2]
        )
        copy.start()
        copies.append(copy)
    for copy in copies:
        copy.wait()


def inside(state, off, coef, act):
    return pl.pallas_call(
        inside_kernel,
        out_shape=(
            jax.ShapeDtypeStruct((OWN, WINDOW, 2 * BLOCK), jnp.bfloat16),
            jax.ShapeDtypeStruct((ROWS, INSIDE), jnp.float32),
            jax.ShapeDtypeStruct((2 * ROWS, INSIDE), jnp.bfloat16),
            jax.ShapeDtypeStruct((ROWS, COLS), jnp.float32),
        ),
        in_specs=[VMEM, VMEM, VMEM, VMEM],
        out_specs=(VMEM, VMEM, VMEM, ANY),
        scratch_shapes=[
            pltpu.VMEM((2 * ROWS, COLS), jnp.bfloat16),
            pltpu.VMEM((1, COLS), jnp.float32),
            pltpu.VMEM((ROWS, COLS - 2 * EDGE), jnp.float32),
            pltpu.SemaphoreType.DMA((OWN - 4,)),
        ],
        compiler_params=params(6),
        cost_estimate=pl.CostEstimate(flops=2_000_000_000, bytes_accessed=4_000_000, transcendentals=0),
        name="inside",
    )(state, off, coef, act)


def advance_kernel(
    state, chip, near, far, coef, act, tables, mid_in, parts2_in, _, out,
    ends, mid_ends, parts, parts2, end_tables, end_off, end_coef, end_act, totals, done, sems,
):
    first, long = on_first_core(), from_far()

    def received(side, rows, cols):
        beside = jnp.where(long, far[rows, cols], near[rows, cols])
        mine = chip[rows, cols]
        return jnp.where(first, beside, mine) if side == 0 else jnp.where(first, mine, beside)

    for side in range(2):
        for part in range(HALO // LANES):
            j = side * (HALO // LANES) + part
            here = slice(part * LANES, (part + 1) * LANES)
            there = slice(HALO + part * LANES, HALO + (part + 1) * LANES)
            lists = received(side, slice(ROWS, SENT), here)
            weights = received(side, slice(ROWS, SENT), there)
            for k in range(KN):
                end_off[k, j : j + 1, :] = lists[k : k + 1, :].astype(jnp.int32)
                end_coef[k, j : j + 1, :] = weights[k : k + 1, :]
            end_act[:, j * LANES : (j + 1) * LANES] = lists[KN : KN + 1, :].astype(jnp.int32)

    def table_of(b, carry):
        build_table(end_tables.at[b], end_off, end_coef, b * (BLOCK // LANES))
        return carry

    lax.fori_loop(0, 2, table_of, 0)
    totals_of(totals, coef, 0, COLS // LANES)
    totals_of(totals, end_coef, COLS, 2 * HALO // LANES)
    parts2[:, 2 * HALO : 2 * HALO + INSIDE] = parts2_in[...]
    every = slice(0, ROWS)
    for side in range(2):
        for start in range(0, EDGE, BLOCK):
            cols = slice(start, start + BLOCK)
            value = received(side, every, cols)
            there = slice(start + side * EDGE, start + side * EDGE + BLOCK)
            ends[side, :, cols] = value
            split_into(parts.at[side], there, value)
            own = slice(start + side * (COLS - EDGE), start + side * (COLS - EDGE) + BLOCK)
            split_into(parts.at[side], slice(start + EDGE - side * EDGE, start + EDGE - side * EDGE + BLOCK), state[:, own])

    def end(side, block, table, centre, total, active):
        value = relaxed(parts.at[side], table, block * BLOCK, centre, total, active)
        mid_ends[side, :, block * BLOCK : (block + 1) * BLOCK] = value
        at = (side * OWN + block) * BLOCK
        split_into(parts2, slice(at, at + BLOCK), value)

    low, high = slice(0, BLOCK), slice(COLS - BLOCK, COLS)
    for side, block in ((0, 0), (1, 1)):
        cols = slice(side * HALO, (side + 1) * HALO)
        centre = ends[side, :, HALO - side * HALO : EDGE - side * HALO]
        end(side, block, end_tables.at[side], centre, totals[:, COLS + side * HALO : COLS + (side + 1) * HALO], end_act[:, cols])
    end(0, 1, tables.at[0], state[:, low], totals[:, low], act[:, low])
    end(1, 0, tables.at[OWN - 1], state[:, high], totals[:, high], act[:, high])
    copies = []
    for at, b in enumerate((0, 1, OWN - 2, OWN - 1)):
        cols = slice(b * BLOCK, (b + 1) * BLOCK)
        if b == 0:
            centre = mid_ends[0, :, BLOCK : 2 * BLOCK]
        elif b == OWN - 1:
            centre = mid_ends[1, :, 0:BLOCK]
        else:
            centre = mid_in[:, (b - 1) * BLOCK : b * BLOCK]
        done[at] = relaxed(parts2, tables.at[b], b * BLOCK, centre, totals[:, cols], act[:, cols])
        copy = pltpu.make_async_copy(done.at[at], out.at[:, pl.ds(b * BLOCK, BLOCK)], sems.at[at])
        copy.start()
        copies.append(copy)
    for copy in copies:
        copy.wait()


def advance(state, chip, near, far, coef, act, tables, mid, parts2, out):
    return pl.pallas_call(
        advance_kernel,
        out_shape=jax.ShapeDtypeStruct((ROWS, COLS), jnp.float32),
        in_specs=[VMEM, VMEM, VMEM, VMEM, VMEM, VMEM, VMEM, VMEM, VMEM, ANY],
        out_specs=ANY,
        scratch_shapes=[
            pltpu.VMEM((2, ROWS, EDGE), jnp.float32),
            pltpu.VMEM((2, ROWS, EDGE), jnp.float32),
            pltpu.VMEM((2, 2 * ROWS, 2 * EDGE), jnp.bfloat16),
            pltpu.VMEM((2 * ROWS, MID), jnp.bfloat16),
            pltpu.VMEM((2, WINDOW, 2 * BLOCK), jnp.bfloat16),
            pltpu.VMEM((KN, 2 * HALO // LANES, LANES), jnp.int32),
            pltpu.VMEM((KN, 2 * HALO // LANES, LANES), jnp.float32),
            pltpu.VMEM((1, 2 * HALO), jnp.int32),
            pltpu.VMEM((1, MID), jnp.float32),
            pltpu.VMEM((4, ROWS, BLOCK), jnp.float32),
            pltpu.SemaphoreType.DMA((4,)),
        ],
        input_output_aliases={9: 0},
        compiler_params=params(12),
        cost_estimate=pl.CostEstimate(flops=4_000_000_000, bytes_accessed=4_000_000, transcendentals=0),
        name="advance",
    )(state, chip, near, far, coef, act, tables, mid, parts2, out)


def couple_kernel(partner, ioff, iweight, act, relax, state, remapped, out, tiles, found_all, sems):
    reads = [
        pltpu.make_async_copy(state.at[pl.ds(LEV * field, 8), :], tiles.at[field], sems.at[field])
        for field in range(NF)
    ]
    for copy in reads:
        copy.start()
    lane = lax.broadcasted_iota(jnp.int32, (KR, LANES), 1)
    for b in range(COLS // LANES):
        cols = slice(b * LANES, (b + 1) * LANES)
        place = ioff[:, cols] + lane + HALO
        chunk = lax.shift_right_logical(place, 7)
        at = jnp.bitwise_and(place, LANES - 1)
        weights = iweight[:, cols]
        for field in range(NF):
            nearby = jnp.zeros((KR, LANES), jnp.float32)
            for q in range(1 + 2 * HALO // LANES):
                source = jnp.broadcast_to(
                    partner[field : field + 1, (b + q) * LANES : (b + q + 1) * LANES], (KR, LANES)
                )
                found = jnp.take_along_axis(source, at, axis=1, mode="promise_in_bounds")
                nearby = jnp.where(chunk == q, found, nearby)
            found_all[field : field + 1, cols] = jnp.sum(weights * nearby, axis=0, keepdims=True)
    writes = [pltpu.make_async_copy(found_all, remapped, sems.at[NF])]
    writes[0].start()
    for field in range(NF):
        reads[field].wait()
        before, value = tiles[field, 0:1, :], found_all[field : field + 1, :]
        tiles[field, 0:1, :] = before + jnp.where(act[...] > 0, relax[0, field] * (value - before), 0.0)
        copy = pltpu.make_async_copy(tiles.at[field], out.at[pl.ds(LEV * field, 8), :], sems.at[field])
        copy.start()
        writes.append(copy)
    for copy in writes:
        copy.wait()


def couple(partner, ioff, iweight, act, relax, state):
    return pl.pallas_call(
        couple_kernel,
        out_shape=(
            jax.ShapeDtypeStruct((NF, COLS), jnp.float32),
            jax.ShapeDtypeStruct((ROWS, COLS), jnp.float32),
        ),
        in_specs=[VMEM, VMEM, VMEM, VMEM, pl.BlockSpec(memory_space=pltpu.SMEM), ANY],
        out_specs=(ANY, ANY),
        scratch_shapes=[
            pltpu.VMEM((NF, 8, COLS), jnp.float32),
            pltpu.VMEM((NF, COLS), jnp.float32),
            pltpu.SemaphoreType.DMA((NF + 1,)),
        ],
        input_output_aliases={5: 1},
        compiler_params=params(4),
        name="couple",
    )(partner, ioff, iweight, act, relax, state)


def body(
    column_state,
    neighbour_offsets,
    edge_coefficients,
    active_levels,
    intersection_offsets,
    intersection_weights,
    relaxation,
):
    count = lax.axis_size("col")
    same_chip = [(i, i ^ 1) for i in range(count)]
    beside = [p for i in range(1, count - 1, 2) for p in ((i, i + 1), (i + 1, i))]
    long = [(i, j) for i, j in beside if i // RUN != j // RUN]
    short = [(i, j) for i, j in beside if i // RUN == j // RUN]
    state = column_state.reshape(ROWS, COLS)
    off = neighbour_offsets.reshape(KN, COLS // LANES, LANES)
    coef = edge_coefficients.reshape(KN, COLS // LANES, LANES)
    sent_beside, sent_chip, surface = pack(state, off, coef, active_levels)
    far = lax.ppermute(sent_beside, "col", long)
    near = lax.ppermute(sent_beside, "col", short)
    chip = lax.ppermute(sent_chip, "col", same_chip)
    tables, mid, parts, out = inside(state, off, coef, active_levels)
    partner = lax.ppermute(widen(chip, near, far, surface), "comp", [(0, 1), (1, 0)])
    advanced = advance(state, chip, near, far, coef, active_levels, tables, mid, parts, out)
    remapped, coupled = couple(
        partner, intersection_offsets[0], intersection_weights[0], active_levels, relaxation, advanced
    )
    return (coupled.reshape(1, NF, LEV, COLS), remapped.reshape(1, NF, COLS))


def solution(mesh):
    return jax.shard_map(
        body,
        mesh=mesh,
        in_specs=(
            P("comp", None, None, "col"),
            P("comp", None, "col"),
            P("comp", None, "col"),
            P("comp", "col"),
            P("comp", None, "col"),
            P("comp", None, "col"),
            P("comp", None),
        ),
        out_specs=(P("comp", None, None, "col"), P("comp", None, "col")),
        check_vma=False,
    )
```

```python
import functools

import jax
import jax.numpy as jnp
from jax import lax
from jax.experimental import pallas as pl
from jax.experimental.pallas import tpu as pltpu
from jax.sharding import PartitionSpec as P

NF = 2
LEV = 80
ROWS = NF * LEV
COLS = 2048
HALO = 256
EDGE = 2 * HALO
KN = 6
KR = 8
BLOCK = 256
WINDOW = BLOCK + 2 * HALO
MID = COLS + 2 * HALO
SENT = ROWS + 8
LANES = 128
PANEL = 16
PACK_MIB = 60
RUN = 12
AHEAD = 4

ANY = pl.BlockSpec(memory_space=pl.ANY)
VMEM = pl.BlockSpec(memory_space=pltpu.VMEM)


def params(mib):
    return pltpu.CompilerParams(vmem_limit_bytes=mib << 20)


def on_first_core():
    return lax.rem(lax.axis_index("col"), 2) == 0


def at_run_end():
    place = lax.rem(lax.axis_index("col"), RUN)
    return jnp.logical_or(place == 0, place == RUN - 1)


def goes_ahead():
    return jnp.logical_and(lax.axis_index("comp") == 0, lax.rem(lax.axis_index("col"), RUN) < AHEAD)


def fill_lists(out, off, coef, act, high):
    out[ROWS + KN : SENT, :] = jnp.zeros((8 - KN, EDGE), jnp.float32)
    for part in range(HALO // LANES):
        j = (COLS - HALO if high else 0) // LANES + part
        here = slice(part * LANES, (part + 1) * LANES)
        there = slice(HALO + part * LANES, HALO + (part + 1) * LANES)
        for k in range(KN):
            out[ROWS + k : ROWS + k + 1, here] = off[k, j : j + 1, :].astype(jnp.float32)
            out[ROWS + k : ROWS + k + 1, there] = coef[k, j : j + 1, :]
        out[ROWS + KN : ROWS + KN + 1, here] = act[:, j * LANES : (j + 1) * LANES].astype(jnp.float32)


def pack_kernel(state, off_in, coef_in, act_in, near, chip, packed, off, coef, act, sems):
    first = on_first_core()
    lists = [
        pltpu.make_async_copy(source, target, sems.at[at])
        for at, (source, target) in enumerate(((off_in, off), (coef_in, coef), (act_in, act)))
    ]
    halves = [pl.ds(half * LEV, LEV) for half in range(NF)]

    def both(run_end, high):
        sides = ((chip, not high),) if run_end else ((near, high), (chip, not high))
        reads, writes = [], []
        for at, (_, upper) in enumerate(sides):
            start = COLS - EDGE if upper else 0
            for half, rows in enumerate(halves):
                reads.append(
                    pltpu.make_async_copy(
                        state.at[rows, pl.ds(start, EDGE)], packed.at[at, rows, :], sems.at[3 + NF * at + half]
                    )
                )
        for copy in reads + lists:
            copy.start()
        for copy in lists:
            copy.wait()
        for at, (out, upper) in enumerate(sides):
            fill_lists(packed.at[at], off, coef, act, upper)
            rows = pl.ds(ROWS, 8)
            copy = pltpu.make_async_copy(packed.at[at, rows, :], out.at[rows, :], sems.at[7 + at])
            copy.start()
            writes.append(copy)
        for at, (out, _) in enumerate(sides):
            for half, rows in enumerate(halves):
                reads[NF * at + half].wait()
                copy = pltpu.make_async_copy(packed.at[at, rows, :], out.at[rows, :], sems.at[9 + NF * at + half])
                copy.start()
                writes.append(copy)
        for copy in writes:
            copy.wait()

    for run_end in (True, False):
        for low in (True, False):

            @pl.when(jnp.logical_and(at_run_end() == run_end, first == low))
            def _(run_end=run_end, low=low):
                both(run_end, not low)


def pack(state, off, coef, act):
    sent = jax.ShapeDtypeStruct((SENT, EDGE), jnp.float32)
    return pl.pallas_call(
        pack_kernel,
        out_shape=(sent, sent),
        in_specs=[ANY, ANY, ANY, ANY],
        out_specs=(ANY, ANY),
        scratch_shapes=[
            pltpu.VMEM((2, SENT, EDGE), jnp.float32),
            pltpu.VMEM(off.shape, off.dtype),
            pltpu.VMEM(coef.shape, coef.dtype),
            pltpu.VMEM(act.shape, act.dtype),
            pltpu.SemaphoreType.DMA((13,)),
        ],
        compiler_params=params(PACK_MIB),
        name="pack",
    )(state, off, coef, act)


def rim_kernel(near, out):
    first = on_first_core()
    for field in range(NF):
        row = slice(LEV * field, LEV * field + 1)
        out[field : field + 1, :] = jnp.where(first, near[row, HALO:EDGE], near[row, 0:HALO])


def rim(near):
    return pl.pallas_call(
        rim_kernel,
        out_shape=jax.ShapeDtypeStruct((NF, HALO), jnp.float32),
        in_specs=[VMEM],
        out_specs=VMEM,
        compiler_params=params(2),
        name="rim",
    )(near)


def widen_kernel(chip, edge, surf, out):
    first = on_first_core()
    out[:, HALO : HALO + COLS] = surf[...]
    for field in range(NF):
        row, this = slice(LEV * field, LEV * field + 1), slice(field, field + 1)
        out[this, 0:HALO] = jnp.where(first, edge[this, :], chip[row, HALO:EDGE])
        out[this, HALO + COLS :] = jnp.where(first, chip[row, 0:HALO], edge[this, :])


def widen(chip, edge, surf):
    return pl.pallas_call(
        widen_kernel,
        out_shape=jax.ShapeDtypeStruct((NF, MID), jnp.float32),
        in_specs=[VMEM, VMEM, VMEM],
        out_specs=VMEM,
        compiler_params=params(2),
        name="widen",
    )(chip, edge, surf)


def build_table(table, off, coef, first_panel):
    for part in range(BLOCK // LANES):
        at = pl.ds(first_panel + part, 1)
        lane = lax.broadcasted_iota(jnp.int32, (PANEL, LANES), 1)
        row = lax.broadcasted_iota(jnp.int32, (PANEL, LANES), 0)
        shift = lane - row + (HALO + part * LANES)
        offs = [jnp.broadcast_to(off[k, at, :], (PANEL, LANES)) for k in range(KN)]
        coefs = [jnp.broadcast_to(coef[k, at, :], (PANEL, LANES)) for k in range(KN)]
        high, low = [], []
        for k in range(KN):
            merged = coefs[k]
            for j in range(KN):
                if j != k:
                    merged = merged + jnp.where(offs[j] == offs[k], coefs[j], 0.0)
            top = merged.astype(jnp.bfloat16)
            high.append(top)
            low.append((merged - top.astype(jnp.float32)).astype(jnp.bfloat16))
        place = [(o + shift).astype(jnp.int16) for o in offs]
        none = jnp.zeros((PANEL, LANES), jnp.bfloat16)
        for start in range(0, WINDOW, PANEL):
            if start + PANEL <= part * LANES or start >= part * LANES + LANES + 2 * HALO:
                first, second = none, none
            else:
                first, second = none, none
                for k in range(KN):
                    hit = place[k] == jnp.int16(start)
                    first = jnp.where(hit, high[k], first)
                    second = jnp.where(hit, low[k], second)
            rows = slice(start, start + PANEL)
            table[rows, part * LANES : (part + 1) * LANES] = first
            table[rows, BLOCK + part * LANES : BLOCK + (part + 1) * LANES] = second


def split_into(parts, cols, value):
    top = value.astype(jnp.bfloat16)
    parts[0:ROWS, cols] = top
    parts[ROWS : 2 * ROWS, cols] = (value - top.astype(jnp.float32)).astype(jnp.bfloat16)


def relaxed(parts, table, start, centre, total, act):
    window = slice(start, start + WINDOW)
    both = jnp.dot(parts[:, window], table[:, 0:BLOCK], preferred_element_type=jnp.float32)
    rest = jnp.dot(parts[0:ROWS, window], table[:, BLOCK:], preferred_element_type=jnp.float32)
    gathered = both[0:ROWS] + both[ROWS:] + rest
    row = lax.broadcasted_iota(jnp.int32, (ROWS, BLOCK), 0)
    level = jnp.where(row >= LEV, row - LEV, row)
    return centre + jnp.where(level < act, gathered - total * centre, 0.0)


INSIDE = COLS - 2 * HALO
CORE = COLS - 2 * EDGE
OWN = COLS // BLOCK


def totals_of(totals, coef, start, count):
    for j in range(count):
        total = coef[0, j : j + 1, :]
        for k in range(1, KN):
            total = total + coef[k, j : j + 1, :]
        totals[:, start + j * LANES : start + (j + 1) * LANES] = total


def inner(state, off, coef, act, tables, mid, parts2, done, parts, totals):
    def table_of(b, carry):
        build_table(tables.at[b], off, coef, b * (BLOCK // LANES))
        return carry

    lax.fori_loop(0, OWN, table_of, 0)
    totals_of(totals, coef, 0, COLS // LANES)
    for b in range(OWN):
        cols = slice(b * BLOCK, (b + 1) * BLOCK)
        split_into(parts, cols, state[:, cols])
    for b in range(1, OWN - 1):
        cols = slice(b * BLOCK, (b + 1) * BLOCK)
        value = relaxed(parts, tables.at[b], (b - 1) * BLOCK, state[:, cols], totals[:, cols], act[:, cols])
        there = slice((b - 1) * BLOCK, b * BLOCK)
        mid[:, there] = value
        split_into(parts2, there, value)
    for b in range(2, OWN - 2):
        cols = slice(b * BLOCK, (b + 1) * BLOCK)
        centre = mid[:, (b - 1) * BLOCK : b * BLOCK]
        here = slice((b - 2) * BLOCK, (b - 1) * BLOCK)
        done[:, here] = relaxed(parts2, tables.at[b], (b - 2) * BLOCK, centre, totals[:, cols], act[:, cols])


INNER = (
    jax.ShapeDtypeStruct((OWN, WINDOW, 2 * BLOCK), jnp.bfloat16),
    jax.ShapeDtypeStruct((ROWS, INSIDE), jnp.float32),
    jax.ShapeDtypeStruct((2 * ROWS, INSIDE), jnp.bfloat16),
    jax.ShapeDtypeStruct((ROWS, CORE), jnp.float32),
)
INNER_SCRATCH = [pltpu.VMEM((2 * ROWS, COLS), jnp.bfloat16), pltpu.VMEM((1, COLS), jnp.float32)]


def inside_kernel(state, off, coef, act, tables, mid, parts2, done, surf, edge, far, parts, totals):
    first = on_first_core()
    for field in range(NF):
        row, this = slice(LEV * field, LEV * field + 1), slice(field, field + 1)
        surf[this, :] = state[row, :]
        edge[this, :] = jnp.where(first, state[row, 0:HALO], state[row, COLS - HALO :])

    for low in (True, False):

        @pl.when(jnp.logical_and(at_run_end(), first == low))
        def _(low=low):
            far[0:ROWS, :] = state[:, 0:EDGE] if low else state[:, COLS - EDGE :]
            fill_lists(far, off, coef, act, not low)

    @pl.when(goes_ahead())
    def _():
        inner(state, off, coef, act, tables, mid, parts2, done, parts, totals)


def inside(state, off, coef, act):
    return pl.pallas_call(
        inside_kernel,
        out_shape=INNER
        + (
            jax.ShapeDtypeStruct((NF, COLS), jnp.float32),
            jax.ShapeDtypeStruct((NF, HALO), jnp.float32),
            jax.ShapeDtypeStruct((SENT, EDGE), jnp.float32),
        ),
        in_specs=[VMEM, VMEM, VMEM, VMEM],
        out_specs=(VMEM,) * 7,
        scratch_shapes=INNER_SCRATCH,
        compiler_params=params(6),
        cost_estimate=pl.CostEstimate(flops=2_000_000_000, bytes_accessed=4_000_000, transcendentals=0),
        name="inside",
    )(state, off, coef, act)


def advance_kernel(
    state, chip, near, far, off, coef, act, tables_in, mid_in, parts_in, core_in, out, done, core_out,
    ends, mid_ends, parts, parts2, end_tables, end_off, end_coef, end_act, totals,
    tables_late, mid_late, parts_late, state_parts, state_totals, sem,
):
    first, run_end, ahead = on_first_core(), at_run_end(), goes_ahead()

    @pl.when(ahead)
    def _():
        core_out[...] = core_in[...]

    @pl.when(jnp.logical_not(ahead))
    def _():
        inner(state, off, coef, act, tables_late, mid_late, parts_late, core_out, state_parts, state_totals)

    write = pltpu.make_async_copy(core_out, out.at[:, pl.ds(EDGE, CORE)], sem)
    write.start()

    def received(side, rows, cols):
        other, mine = jnp.where(run_end, far[rows, cols], near[rows, cols]), chip[rows, cols]
        return jnp.where(first, other, mine) if side == 0 else jnp.where(first, mine, other)

    for side in range(2):
        for part in range(HALO // LANES):
            j = side * (HALO // LANES) + part
            here = slice(part * LANES, (part + 1) * LANES)
            there = slice(HALO + part * LANES, HALO + (part + 1) * LANES)
            lists = received(side, slice(ROWS, SENT), here)
            weights = received(side, slice(ROWS, SENT), there)
            for k in range(KN):
                end_off[k, j : j + 1, :] = lists[k : k + 1, :].astype(jnp.int32)
                end_coef[k, j : j + 1, :] = weights[k : k + 1, :]
            end_act[:, j * LANES : (j + 1) * LANES] = lists[KN : KN + 1, :].astype(jnp.int32)

    def table_of(b, carry):
        build_table(end_tables.at[b], end_off, end_coef, b * (BLOCK // LANES))
        return carry

    lax.fori_loop(0, 2, table_of, 0)
    totals_of(totals, coef, 0, COLS // LANES)
    totals_of(totals, end_coef, COLS, 2 * HALO // LANES)
    every = slice(0, ROWS)
    for side in range(2):
        for start in range(0, EDGE, BLOCK):
            cols = slice(start, start + BLOCK)
            value = received(side, every, cols)
            there = slice(start + side * EDGE, start + side * EDGE + BLOCK)
            ends[side, :, cols] = value
            split_into(parts.at[side], there, value)
            own = slice(start + side * (COLS - EDGE), start + side * (COLS - EDGE) + BLOCK)
            split_into(parts.at[side], slice(start + EDGE - side * EDGE, start + EDGE - side * EDGE + BLOCK), state[:, own])

    def end(side, block, table, centre, total, active):
        value = relaxed(parts.at[side], table, block * BLOCK, centre, total, active)
        mid_ends[side, :, block * BLOCK : (block + 1) * BLOCK] = value
        at = (side * OWN + block) * BLOCK
        split_into(parts2, slice(at, at + BLOCK), value)

    low, high = slice(0, BLOCK), slice(COLS - BLOCK, COLS)

    def finish(tables, mid, parts_mid):
        parts2[:, 2 * HALO : 2 * HALO + INSIDE] = parts_mid[...]
        for side, block in ((0, 0), (1, 1)):
            cols = slice(side * HALO, (side + 1) * HALO)
            centre = ends[side, :, HALO - side * HALO : EDGE - side * HALO]
            total = totals[:, COLS + side * HALO : COLS + (side + 1) * HALO]
            end(side, block, end_tables.at[side], centre, total, end_act[:, cols])
        end(0, 1, tables.at[0], state[:, low], totals[:, low], act[:, low])
        end(1, 0, tables.at[OWN - 1], state[:, high], totals[:, high], act[:, high])
        for at, b in enumerate((0, 1, OWN - 2, OWN - 1)):
            cols = slice(b * BLOCK, (b + 1) * BLOCK)
            if b == 0:
                centre = mid_ends[0, :, BLOCK : 2 * BLOCK]
            elif b == OWN - 1:
                centre = mid_ends[1, :, 0:BLOCK]
            else:
                centre = mid[:, (b - 1) * BLOCK : b * BLOCK]
            there = slice(at * BLOCK, (at + 1) * BLOCK)
            done[:, there] = relaxed(parts2, tables.at[b], b * BLOCK, centre, totals[:, cols], act[:, cols])

    @pl.when(ahead)
    def _():
        finish(tables_in, mid_in, parts_in)

    @pl.when(jnp.logical_not(ahead))
    def _():
        finish(tables_late, mid_late, parts_late)

    write.wait()


def advance(state, chip, near, far, off, coef, act, tables, mid, parts2, core):
    return pl.pallas_call(
        advance_kernel,
        out_shape=(
            jax.ShapeDtypeStruct((ROWS, COLS), jnp.float32),
            jax.ShapeDtypeStruct((ROWS, 2 * EDGE), jnp.float32),
            jax.ShapeDtypeStruct((ROWS, CORE), jnp.float32),
        ),
        in_specs=[VMEM] * 11,
        out_specs=(ANY, VMEM, VMEM),
        scratch_shapes=[
            pltpu.VMEM((2, ROWS, EDGE), jnp.float32),
            pltpu.VMEM((2, ROWS, EDGE), jnp.float32),
            pltpu.VMEM((2, 2 * ROWS, 2 * EDGE), jnp.bfloat16),
            pltpu.VMEM((2 * ROWS, MID), jnp.bfloat16),
            pltpu.VMEM((2, WINDOW, 2 * BLOCK), jnp.bfloat16),
            pltpu.VMEM((KN, 2 * HALO // LANES, LANES), jnp.int32),
            pltpu.VMEM((KN, 2 * HALO // LANES, LANES), jnp.float32),
            pltpu.VMEM((1, 2 * HALO), jnp.int32),
            pltpu.VMEM((1, MID), jnp.float32),
        ]
        + [pltpu.VMEM(kept.shape, kept.dtype) for kept in INNER[:3]]
        + INNER_SCRATCH
        + [pltpu.SemaphoreType.DMA],
        compiler_params=params(24),
        cost_estimate=pl.CostEstimate(flops=6_000_000_000, bytes_accessed=4_000_000, transcendentals=0),
        name="advance",
    )(state, chip, near, far, off, coef, act, tables, mid, parts2, core)


def couple_kernel(got, beyond, ioff, iweight, act, relax, core, ends, _, remapped, out, partner, tiles, found_all, sems):
    writes = []
    for side in range(2):
        for field in range(NF):
            rows = pl.ds(LEV * field + 8, LEV - 8)
            writes.append(
                pltpu.make_async_copy(
                    ends.at[rows, pl.ds(side * EDGE, EDGE)],
                    out.at[rows, pl.ds(side * (COLS - EDGE), EDGE)],
                    sems.at[NF * side + field],
                )
            )
    for copy in writes:
        copy.start()
    first, run_end = on_first_core(), at_run_end()
    left, right = slice(0, HALO), slice(HALO + COLS, MID)
    partner[:, HALO : HALO + COLS] = got[:, HALO : HALO + COLS]
    partner[:, left] = jnp.where(jnp.logical_and(run_end, first), beyond[...], got[:, left])
    partner[:, right] = jnp.where(jnp.logical_and(run_end, jnp.logical_not(first)), beyond[...], got[:, right])
    lane = lax.broadcasted_iota(jnp.int32, (KR, LANES), 1)
    for b in range(COLS // LANES):
        cols = slice(b * LANES, (b + 1) * LANES)
        place = ioff[:, cols] + lane + HALO
        chunk = lax.shift_right_logical(place, 7)
        at = jnp.bitwise_and(place, LANES - 1)
        weights = iweight[:, cols]
        for field in range(NF):
            nearby = jnp.zeros((KR, LANES), jnp.float32)
            for q in range(1 + 2 * HALO // LANES):
                source = jnp.broadcast_to(
                    partner[field : field + 1, (b + q) * LANES : (b + q + 1) * LANES], (KR, LANES)
                )
                found = jnp.take_along_axis(source, at, axis=1, mode="promise_in_bounds")
                nearby = jnp.where(chunk == q, found, nearby)
            found_all[field : field + 1, cols] = jnp.sum(weights * nearby, axis=0, keepdims=True)
    copy = pltpu.make_async_copy(found_all, remapped, sems.at[2 * NF])
    copy.start()
    writes.append(copy)
    for field in range(NF):
        rows = slice(LEV * field, LEV * field + 8)
        tiles[field, :, 0:EDGE] = ends[rows, 0:EDGE]
        tiles[field, :, EDGE : EDGE + CORE] = core[rows, :]
        tiles[field, :, EDGE + CORE :] = ends[rows, EDGE:]
        before, value = tiles[field, 0:1, :], found_all[field : field + 1, :]
        tiles[field, 0:1, :] = before + jnp.where(act[...] > 0, relax[0, field] * (value - before), 0.0)
        copy = pltpu.make_async_copy(
            tiles.at[field], out.at[pl.ds(LEV * field, 8), :], sems.at[2 * NF + 1 + field]
        )
        copy.start()
        writes.append(copy)
    for copy in writes:
        copy.wait()


def couple(partner, beyond, ioff, iweight, act, relax, core, ends, out):
    return pl.pallas_call(
        couple_kernel,
        out_shape=(
            jax.ShapeDtypeStruct((NF, COLS), jnp.float32),
            jax.ShapeDtypeStruct((ROWS, COLS), jnp.float32),
        ),
        in_specs=[VMEM, VMEM, VMEM, VMEM, VMEM, pl.BlockSpec(memory_space=pltpu.SMEM), VMEM, VMEM, ANY],
        out_specs=(ANY, ANY),
        scratch_shapes=[
            pltpu.VMEM((NF, MID), jnp.float32),
            pltpu.VMEM((NF, 8, COLS), jnp.float32),
            pltpu.VMEM((NF, COLS), jnp.float32),
            pltpu.SemaphoreType.DMA((3 * NF + 1,)),
        ],
        input_output_aliases={8: 1},
        compiler_params=params(4),
        name="couple",
    )(partner, beyond, ioff, iweight, act, relax, core, ends, out)


def body(
    column_state,
    neighbour_offsets,
    edge_coefficients,
    active_levels,
    intersection_offsets,
    intersection_weights,
    relaxation,
):
    count = lax.axis_size("col")
    same_chip = [(i, i ^ 1) for i in range(count)]
    pairs = [p for i in range(1, count - 1, 2) for p in ((i, i + 1), (i + 1, i))]
    long = [(i, j) for i, j in pairs if i // RUN != j // RUN]
    short = [(i, j) for i, j in pairs if i // RUN == j // RUN]
    across = [(c * count + i, (1 - c) * count + j) for c in range(2) for i, j in long]
    state = column_state.reshape(ROWS, COLS)
    off = neighbour_offsets.reshape(KN, COLS // LANES, LANES)
    coef = edge_coefficients.reshape(KN, COLS // LANES, LANES)
    near, chip = pack(state, off, coef, active_levels)
    chip = lax.ppermute(chip, "col", same_chip)
    near = lax.ppermute(near, "col", short)
    tables, mid, parts, core, surface, edge, far = inside(state, off, coef, active_levels)
    far = lax.ppermute(far, "col", long)
    beyond = lax.ppermute(edge, ("comp", "col"), across)
    partner = lax.ppermute(widen(chip, rim(near), surface), "comp", [(0, 1), (1, 0)])
    out, ends, core = advance(state, chip, near, far, off, coef, active_levels, tables, mid, parts, core)
    remapped, coupled = couple(
        partner, beyond, intersection_offsets[0], intersection_weights[0], active_levels, relaxation, core, ends, out
    )
    return (coupled.reshape(1, NF, LEV, COLS), remapped.reshape(1, NF, COLS))


def solution(mesh):
    return jax.shard_map(
        body,
        mesh=mesh,
        in_specs=(
            P("comp", None, None, "col"),
            P("comp", None, "col"),
            P("comp", None, "col"),
            P("comp", "col"),
            P("comp", None, "col"),
            P("comp", None, "col"),
            P("comp", None),
        ),
        out_specs=(P("comp", None, None, "col"), P("comp", None, "col")),
        check_vma=False,
    )
```

```python
import functools

import jax
import jax.numpy as jnp
from jax import lax
from jax.experimental import pallas as pl
from jax.experimental.pallas import tpu as pltpu
from jax.sharding import PartitionSpec as P

NF = 2
LEV = 80
ROWS = NF * LEV
COLS = 2048
HALO = 256
EDGE = 2 * HALO
KN = 6
KR = 8
BLOCK = 256
WINDOW = BLOCK + 2 * HALO
MID = COLS + 2 * HALO
SENT = ROWS + 8
LANES = 128
PANEL = 16
RUN = 12
AHEAD = 4

ANY = pl.BlockSpec(memory_space=pl.ANY)
VMEM = pl.BlockSpec(memory_space=pltpu.VMEM)


def params(mib):
    return pltpu.CompilerParams(vmem_limit_bytes=mib << 20)


def on_first_core():
    return lax.rem(lax.axis_index("col"), 2) == 0


def at_run_end():
    place = lax.rem(lax.axis_index("col"), RUN)
    return jnp.logical_or(place == 0, place == RUN - 1)


def goes_ahead():
    return jnp.logical_and(lax.axis_index("comp") == 0, lax.rem(lax.axis_index("col"), RUN) < AHEAD)


def fill_lists(out, off, coef, act, high):
    out[ROWS + KN : SENT, :] = jnp.zeros((8 - KN, EDGE), jnp.float32)
    for part in range(HALO // LANES):
        j = (COLS - HALO if high else 0) // LANES + part
        here = slice(part * LANES, (part + 1) * LANES)
        there = slice(HALO + part * LANES, HALO + (part + 1) * LANES)
        for k in range(KN):
            out[ROWS + k : ROWS + k + 1, here] = off[k, j : j + 1, :].astype(jnp.float32)
            out[ROWS + k : ROWS + k + 1, there] = coef[k, j : j + 1, :]
        out[ROWS + KN : ROWS + KN + 1, here] = act[:, j * LANES : (j + 1) * LANES].astype(jnp.float32)


def begin_kernel(out):
    out[...] = jnp.zeros(out.shape, out.dtype)


def begin():
    return pl.pallas_call(
        begin_kernel,
        out_shape=jax.ShapeDtypeStruct((8, LANES), jnp.float32),
        out_specs=VMEM,
        compiler_params=params(1),
        cost_estimate=pl.CostEstimate(flops=4_000_000_000, bytes_accessed=8_000_000, transcendentals=0),
        name="begin",
    )()


def pack_kernel(_, state, off, coef, act, near, chip):
    first = on_first_core()

    def both(run_end, high):
        for out, upper in ((chip, not high),) if run_end else ((chip, not high), (near, high)):
            start = COLS - EDGE if upper else 0
            out[0:ROWS, :] = state[:, start : start + EDGE]
            fill_lists(out, off, coef, act, upper)

    for run_end in (True, False):
        for low in (True, False):

            @pl.when(jnp.logical_and(at_run_end() == run_end, first == low))
            def _(run_end=run_end, low=low):
                both(run_end, not low)


def pack(state, off, coef, act):
    sent = jax.ShapeDtypeStruct((SENT, EDGE), jnp.float32)
    return pl.pallas_call(
        pack_kernel,
        out_shape=(sent, sent),
        in_specs=[VMEM] * 5,
        out_specs=(VMEM, VMEM),
        compiler_params=params(2),
        name="pack",
    )(begin(), state, off, coef, act)


def rim_kernel(near, out):
    first = on_first_core()
    for field in range(NF):
        row = slice(LEV * field, LEV * field + 1)
        out[field : field + 1, :] = jnp.where(first, near[row, HALO:EDGE], near[row, 0:HALO])


def rim(near):
    return pl.pallas_call(
        rim_kernel,
        out_shape=jax.ShapeDtypeStruct((NF, HALO), jnp.float32),
        in_specs=[VMEM],
        out_specs=VMEM,
        compiler_params=params(2),
        name="rim",
    )(near)


def widen_kernel(chip, edge, surf, out):
    first = on_first_core()
    out[:, HALO : HALO + COLS] = surf[...]
    for field in range(NF):
        row, this = slice(LEV * field, LEV * field + 1), slice(field, field + 1)
        out[this, 0:HALO] = jnp.where(first, edge[this, :], chip[row, HALO:EDGE])
        out[this, HALO + COLS :] = jnp.where(first, chip[row, 0:HALO], edge[this, :])


def widen(chip, edge, surf):
    return pl.pallas_call(
        widen_kernel,
        out_shape=jax.ShapeDtypeStruct((NF, MID), jnp.float32),
        in_specs=[VMEM, VMEM, VMEM],
        out_specs=VMEM,
        compiler_params=params(2),
        name="widen",
    )(chip, edge, surf)


def build_table(table, off, coef, first_panel):
    for part in range(BLOCK // LANES):
        at = pl.ds(first_panel + part, 1)
        lane = lax.broadcasted_iota(jnp.int32, (PANEL, LANES), 1)
        row = lax.broadcasted_iota(jnp.int32, (PANEL, LANES), 0)
        shift = lane - row + (HALO + part * LANES)
        offs = [jnp.broadcast_to(off[k, at, :], (PANEL, LANES)) for k in range(KN)]
        coefs = [jnp.broadcast_to(coef[k, at, :], (PANEL, LANES)) for k in range(KN)]
        high, low = [], []
        for k in range(KN):
            merged = coefs[k]
            for j in range(KN):
                if j != k:
                    merged = merged + jnp.where(offs[j] == offs[k], coefs[j], 0.0)
            top = merged.astype(jnp.bfloat16)
            high.append(top)
            low.append((merged - top.astype(jnp.float32)).astype(jnp.bfloat16))
        place = [(o + shift).astype(jnp.int16) for o in offs]
        none = jnp.zeros((PANEL, LANES), jnp.bfloat16)
        for start in range(0, WINDOW, PANEL):
            if start + PANEL <= part * LANES or start >= part * LANES + LANES + 2 * HALO:
                first, second = none, none
            else:
                first, second = none, none
                for k in range(KN):
                    hit = place[k] == jnp.int16(start)
                    first = jnp.where(hit, high[k], first)
                    second = jnp.where(hit, low[k], second)
            rows = slice(start, start + PANEL)
            table[rows, part * LANES : (part + 1) * LANES] = first
            table[rows, BLOCK + part * LANES : BLOCK + (part + 1) * LANES] = second


def split_into(parts, cols, value):
    top = value.astype(jnp.bfloat16)
    parts[0:ROWS, cols] = top
    parts[ROWS : 2 * ROWS, cols] = (value - top.astype(jnp.float32)).astype(jnp.bfloat16)


def relaxed(parts, table, start, centre, total, act):
    window = slice(start, start + WINDOW)
    both = jnp.dot(parts[:, window], table[:, 0:BLOCK], preferred_element_type=jnp.float32)
    rest = jnp.dot(parts[0:ROWS, window], table[:, BLOCK:], preferred_element_type=jnp.float32)
    gathered = both[0:ROWS] + both[ROWS:] + rest
    row = lax.broadcasted_iota(jnp.int32, (ROWS, BLOCK), 0)
    level = jnp.where(row >= LEV, row - LEV, row)
    return centre + jnp.where(level < act, gathered - total * centre, 0.0)


INSIDE = COLS - 2 * HALO
CORE = COLS - 2 * EDGE
OWN = COLS // BLOCK


def totals_of(totals, coef, start, count):
    for j in range(count):
        total = coef[0, j : j + 1, :]
        for k in range(1, KN):
            total = total + coef[k, j : j + 1, :]
        totals[:, start + j * LANES : start + (j + 1) * LANES] = total


def inner(state, off, coef, act, tables, mid, parts2, done, parts, totals):
    def table_of(b, carry):
        build_table(tables.at[b], off, coef, b * (BLOCK // LANES))
        return carry

    lax.fori_loop(0, OWN, table_of, 0)
    totals_of(totals, coef, 0, COLS // LANES)
    for b in range(OWN):
        cols = slice(b * BLOCK, (b + 1) * BLOCK)
        split_into(parts, cols, state[:, cols])
    for b in range(1, OWN - 1):
        cols = slice(b * BLOCK, (b + 1) * BLOCK)
        value = relaxed(parts, tables.at[b], (b - 1) * BLOCK, state[:, cols], totals[:, cols], act[:, cols])
        there = slice((b - 1) * BLOCK, b * BLOCK)
        mid[:, there] = value
        split_into(parts2, there, value)
    for b in range(2, OWN - 2):
        cols = slice(b * BLOCK, (b + 1) * BLOCK)
        centre = mid[:, (b - 1) * BLOCK : b * BLOCK]
        here = slice((b - 2) * BLOCK, (b - 1) * BLOCK)
        done[:, here] = relaxed(parts2, tables.at[b], (b - 2) * BLOCK, centre, totals[:, cols], act[:, cols])


INNER = (
    jax.ShapeDtypeStruct((OWN, WINDOW, 2 * BLOCK), jnp.bfloat16),
    jax.ShapeDtypeStruct((ROWS, INSIDE), jnp.float32),
    jax.ShapeDtypeStruct((2 * ROWS, INSIDE), jnp.bfloat16),
    jax.ShapeDtypeStruct((ROWS, CORE), jnp.float32),
)
INNER_SCRATCH = [pltpu.VMEM((2 * ROWS, COLS), jnp.bfloat16), pltpu.VMEM((1, COLS), jnp.float32)]


def inside_kernel(state, off, coef, act, tables, mid, parts2, done, surf, edge, far, parts, totals):
    first = on_first_core()
    for field in range(NF):
        row, this = slice(LEV * field, LEV * field + 1), slice(field, field + 1)
        surf[this, :] = state[row, :]
        edge[this, :] = jnp.where(first, state[row, 0:HALO], state[row, COLS - HALO :])

    for low in (True, False):

        @pl.when(jnp.logical_and(at_run_end(), first == low))
        def _(low=low):
            far[0:ROWS, :] = state[:, 0:EDGE] if low else state[:, COLS - EDGE :]
            fill_lists(far, off, coef, act, not low)

    @pl.when(goes_ahead())
    def _():
        inner(state, off, coef, act, tables, mid, parts2, done, parts, totals)


def inside(state, off, coef, act):
    return pl.pallas_call(
        inside_kernel,
        out_shape=INNER
        + (
            jax.ShapeDtypeStruct((NF, COLS), jnp.float32),
            jax.ShapeDtypeStruct((NF, HALO), jnp.float32),
            jax.ShapeDtypeStruct((SENT, EDGE), jnp.float32),
        ),
        in_specs=[VMEM, VMEM, VMEM, VMEM],
        out_specs=(VMEM,) * 7,
        scratch_shapes=INNER_SCRATCH,
        compiler_params=params(6),
        cost_estimate=pl.CostEstimate(flops=2_000_000_000, bytes_accessed=4_000_000, transcendentals=0),
        name="inside",
    )(state, off, coef, act)


def advance_kernel(
    state, chip, near, far, off, coef, act, tables_in, mid_in, parts_in, core_in, out, done, core_out,
    ends, mid_ends, parts, parts2, end_tables, end_off, end_coef, end_act, totals,
    tables_late, mid_late, parts_late, state_parts, state_totals, sem,
):
    first, run_end, ahead = on_first_core(), at_run_end(), goes_ahead()

    @pl.when(ahead)
    def _():
        core_out[...] = core_in[...]

    @pl.when(jnp.logical_not(ahead))
    def _():
        inner(state, off, coef, act, tables_late, mid_late, parts_late, core_out, state_parts, state_totals)

    write = pltpu.make_async_copy(core_out, out.at[:, pl.ds(EDGE, CORE)], sem)
    write.start()

    def received(side, rows, cols):
        other, mine = jnp.where(run_end, far[rows, cols], near[rows, cols]), chip[rows, cols]
        return jnp.where(first, other, mine) if side == 0 else jnp.where(first, mine, other)

    for side in range(2):
        for part in range(HALO // LANES):
            j = side * (HALO // LANES) + part
            here = slice(part * LANES, (part + 1) * LANES)
            there = slice(HALO + part * LANES, HALO + (part + 1) * LANES)
            lists = received(side, slice(ROWS, SENT), here)
            weights = received(side, slice(ROWS, SENT), there)
            for k in range(KN):
                end_off[k, j : j + 1, :] = lists[k : k + 1, :].astype(jnp.int32)
                end_coef[k, j : j + 1, :] = weights[k : k + 1, :]
            end_act[:, j * LANES : (j + 1) * LANES] = lists[KN : KN + 1, :].astype(jnp.int32)

    def table_of(b, carry):
        build_table(end_tables.at[b], end_off, end_coef, b * (BLOCK // LANES))
        return carry

    lax.fori_loop(0, 2, table_of, 0)
    totals_of(totals, coef, 0, COLS // LANES)
    totals_of(totals, end_coef, COLS, 2 * HALO // LANES)
    every = slice(0, ROWS)
    for side in range(2):
        for start in range(0, EDGE, BLOCK):
            cols = slice(start, start + BLOCK)
            value = received(side, every, cols)
            there = slice(start + side * EDGE, start + side * EDGE + BLOCK)
            ends[side, :, cols] = value
            split_into(parts.at[side], there, value)
            own = slice(start + side * (COLS - EDGE), start + side * (COLS - EDGE) + BLOCK)
            split_into(parts.at[side], slice(start + EDGE - side * EDGE, start + EDGE - side * EDGE + BLOCK), state[:, own])

    def end(side, block, table, centre, total, active):
        value = relaxed(parts.at[side], table, block * BLOCK, centre, total, active)
        mid_ends[side, :, block * BLOCK : (block + 1) * BLOCK] = value
        at = (side * OWN + block) * BLOCK
        split_into(parts2, slice(at, at + BLOCK), value)

    low, high = slice(0, BLOCK), slice(COLS - BLOCK, COLS)

    def finish(tables, mid, parts_mid):
        parts2[:, 2 * HALO : 2 * HALO + INSIDE] = parts_mid[...]
        for side, block in ((0, 0), (1, 1)):
            cols = slice(side * HALO, (side + 1) * HALO)
            centre = ends[side, :, HALO - side * HALO : EDGE - side * HALO]
            total = totals[:, COLS + side * HALO : COLS + (side + 1) * HALO]
            end(side, block, end_tables.at[side], centre, total, end_act[:, cols])
        end(0, 1, tables.at[0], state[:, low], totals[:, low], act[:, low])
        end(1, 0, tables.at[OWN - 1], state[:, high], totals[:, high], act[:, high])
        for at, b in enumerate((0, 1, OWN - 2, OWN - 1)):
            cols = slice(b * BLOCK, (b + 1) * BLOCK)
            if b == 0:
                centre = mid_ends[0, :, BLOCK : 2 * BLOCK]
            elif b == OWN - 1:
                centre = mid_ends[1, :, 0:BLOCK]
            else:
                centre = mid[:, (b - 1) * BLOCK : b * BLOCK]
            there = slice(at * BLOCK, (at + 1) * BLOCK)
            done[:, there] = relaxed(parts2, tables.at[b], b * BLOCK, centre, totals[:, cols], act[:, cols])

    @pl.when(ahead)
    def _():
        finish(tables_in, mid_in, parts_in)

    @pl.when(jnp.logical_not(ahead))
    def _():
        finish(tables_late, mid_late, parts_late)

    write.wait()


def advance(state, chip, near, far, off, coef, act, tables, mid, parts2, core):
    return pl.pallas_call(
        advance_kernel,
        out_shape=(
            jax.ShapeDtypeStruct((ROWS, COLS), jnp.float32),
            jax.ShapeDtypeStruct((ROWS, 2 * EDGE), jnp.float32),
            jax.ShapeDtypeStruct((ROWS, CORE), jnp.float32),
        ),
        in_specs=[VMEM] * 11,
        out_specs=(ANY, VMEM, VMEM),
        scratch_shapes=[
            pltpu.VMEM((2, ROWS, EDGE), jnp.float32),
            pltpu.VMEM((2, ROWS, EDGE), jnp.float32),
            pltpu.VMEM((2, 2 * ROWS, 2 * EDGE), jnp.bfloat16),
            pltpu.VMEM((2 * ROWS, MID), jnp.bfloat16),
            pltpu.VMEM((2, WINDOW, 2 * BLOCK), jnp.bfloat16),
            pltpu.VMEM((KN, 2 * HALO // LANES, LANES), jnp.int32),
            pltpu.VMEM((KN, 2 * HALO // LANES, LANES), jnp.float32),
            pltpu.VMEM((1, 2 * HALO), jnp.int32),
            pltpu.VMEM((1, MID), jnp.float32),
        ]
        + [pltpu.VMEM(kept.shape, kept.dtype) for kept in INNER[:3]]
        + INNER_SCRATCH
        + [pltpu.SemaphoreType.DMA],
        compiler_params=params(24),
        cost_estimate=pl.CostEstimate(flops=6_000_000_000, bytes_accessed=4_000_000, transcendentals=0),
        name="advance",
    )(state, chip, near, far, off, coef, act, tables, mid, parts2, core)


def couple_kernel(got, beyond, ioff, iweight, act, relax, core, ends, _, remapped, out, partner, tiles, found_all, sems):
    writes = []
    for side in range(2):
        for field in range(NF):
            rows = pl.ds(LEV * field + 8, LEV - 8)
            writes.append(
                pltpu.make_async_copy(
                    ends.at[rows, pl.ds(side * EDGE, EDGE)],
                    out.at[rows, pl.ds(side * (COLS - EDGE), EDGE)],
                    sems.at[NF * side + field],
                )
            )
    for copy in writes:
        copy.start()
    first, run_end = on_first_core(), at_run_end()
    left, right = slice(0, HALO), slice(HALO + COLS, MID)
    partner[:, HALO : HALO + COLS] = got[:, HALO : HALO + COLS]
    partner[:, left] = jnp.where(jnp.logical_and(run_end, first), beyond[...], got[:, left])
    partner[:, right] = jnp.where(jnp.logical_and(run_end, jnp.logical_not(first)), beyond[...], got[:, right])
    lane = lax.broadcasted_iota(jnp.int32, (KR, LANES), 1)
    for b in range(COLS // LANES):
        cols = slice(b * LANES, (b + 1) * LANES)
        place = ioff[:, cols] + lane + HALO
        chunk = lax.shift_right_logical(place, 7)
        at = jnp.bitwise_and(place, LANES - 1)
        weights = iweight[:, cols]
        for field in range(NF):
            nearby = jnp.zeros((KR, LANES), jnp.float32)
            for q in range(1 + 2 * HALO // LANES):
                source = jnp.broadcast_to(
                    partner[field : field + 1, (b + q) * LANES : (b + q + 1) * LANES], (KR, LANES)
                )
                found = jnp.take_along_axis(source, at, axis=1, mode="promise_in_bounds")
                nearby = jnp.where(chunk == q, found, nearby)
            found_all[field : field + 1, cols] = jnp.sum(weights * nearby, axis=0, keepdims=True)
    copy = pltpu.make_async_copy(found_all, remapped, sems.at[2 * NF])
    copy.start()
    writes.append(copy)
    for field in range(NF):
        rows = slice(LEV * field, LEV * field + 8)
        tiles[field, :, 0:EDGE] = ends[rows, 0:EDGE]
        tiles[field, :, EDGE : EDGE + CORE] = core[rows, :]
        tiles[field, :, EDGE + CORE :] = ends[rows, EDGE:]
        before, value = tiles[field, 0:1, :], found_all[field : field + 1, :]
        tiles[field, 0:1, :] = before + jnp.where(act[...] > 0, relax[0, field] * (value - before), 0.0)
        copy = pltpu.make_async_copy(
            tiles.at[field], out.at[pl.ds(LEV * field, 8), :], sems.at[2 * NF + 1 + field]
        )
        copy.start()
        writes.append(copy)
    for copy in writes:
        copy.wait()


def couple(partner, beyond, ioff, iweight, act, relax, core, ends, out):
    return pl.pallas_call(
        couple_kernel,
        out_shape=(
            jax.ShapeDtypeStruct((NF, COLS), jnp.float32),
            jax.ShapeDtypeStruct((ROWS, COLS), jnp.float32),
        ),
        in_specs=[VMEM, VMEM, VMEM, VMEM, VMEM, pl.BlockSpec(memory_space=pltpu.SMEM), VMEM, VMEM, ANY],
        out_specs=(ANY, ANY),
        scratch_shapes=[
            pltpu.VMEM((NF, MID), jnp.float32),
            pltpu.VMEM((NF, 8, COLS), jnp.float32),
            pltpu.VMEM((NF, COLS), jnp.float32),
            pltpu.SemaphoreType.DMA((3 * NF + 1,)),
        ],
        input_output_aliases={8: 1},
        compiler_params=params(4),
        name="couple",
    )(partner, beyond, ioff, iweight, act, relax, core, ends, out)


def body(
    column_state,
    neighbour_offsets,
    edge_coefficients,
    active_levels,
    intersection_offsets,
    intersection_weights,
    relaxation,
):
    count = lax.axis_size("col")
    same_chip = [(i, i ^ 1) for i in range(count)]
    pairs = [p for i in range(1, count - 1, 2) for p in ((i, i + 1), (i + 1, i))]
    long = [(i, j) for i, j in pairs if i // RUN != j // RUN]
    short = [(i, j) for i, j in pairs if i // RUN == j // RUN]
    across = [(c * count + i, (1 - c) * count + j) for c in range(2) for i, j in long]
    state = column_state.reshape(ROWS, COLS)
    off = neighbour_offsets.reshape(KN, COLS // LANES, LANES)
    coef = edge_coefficients.reshape(KN, COLS // LANES, LANES)
    near, chip = pack(state, off, coef, active_levels)
    chip = lax.ppermute(chip, "col", same_chip)
    near = lax.ppermute(near, "col", short)
    tables, mid, parts, core, surface, edge, far = inside(state, off, coef, active_levels)
    far = lax.ppermute(far, "col", long)
    beyond = lax.ppermute(edge, ("comp", "col"), across)
    partner = lax.ppermute(widen(chip, rim(near), surface), "comp", [(0, 1), (1, 0)])
    out, ends, core = advance(state, chip, near, far, off, coef, active_levels, tables, mid, parts, core)
    remapped, coupled = couple(
        partner, beyond, intersection_offsets[0], intersection_weights[0], active_levels, relaxation, core, ends, out
    )
    return (coupled.reshape(1, NF, LEV, COLS), remapped.reshape(1, NF, COLS))


def solution(mesh):
    return jax.shard_map(
        body,
        mesh=mesh,
        in_specs=(
            P("comp", None, None, "col"),
            P("comp", None, "col"),
            P("comp", None, "col"),
            P("comp", "col"),
            P("comp", None, "col"),
            P("comp", None, "col"),
            P("comp", None),
        ),
        out_specs=(P("comp", None, None, "col"), P("comp", None, "col")),
        check_vma=False,
    )
```

```python
import functools

import jax
import jax.numpy as jnp
from jax import lax
from jax.experimental import pallas as pl
from jax.experimental.pallas import tpu as pltpu
from jax.sharding import PartitionSpec as P

NF = 2
LEV = 80
ROWS = NF * LEV
COLS = 2048
HALO = 256
EDGE = 2 * HALO
KN = 6
KR = 8
BLOCK = 256
WINDOW = BLOCK + 2 * HALO
MID = COLS + 2 * HALO
SENT = ROWS + 8
LANES = 128
PANEL = 16
RUN = 12
AHEAD = 4

ANY = pl.BlockSpec(memory_space=pl.ANY)
VMEM = pl.BlockSpec(memory_space=pltpu.VMEM)


def params(mib):
    return pltpu.CompilerParams(vmem_limit_bytes=mib << 20)


def on_first_core():
    return lax.rem(lax.axis_index("col"), 2) == 0


def at_run_end():
    place = lax.rem(lax.axis_index("col"), RUN)
    return jnp.logical_or(place == 0, place == RUN - 1)


def goes_ahead():
    return jnp.logical_and(lax.axis_index("comp") == 0, lax.rem(lax.axis_index("col"), RUN) < AHEAD)


def fill_lists(out, off, coef, act, high):
    out[ROWS + KN : SENT, :] = jnp.zeros((8 - KN, EDGE), jnp.float32)
    for part in range(HALO // LANES):
        j = (COLS - HALO if high else 0) // LANES + part
        here = slice(part * LANES, (part + 1) * LANES)
        there = slice(HALO + part * LANES, HALO + (part + 1) * LANES)
        for k in range(KN):
            out[ROWS + k : ROWS + k + 1, here] = off[k, j : j + 1, :].astype(jnp.float32)
            out[ROWS + k : ROWS + k + 1, there] = coef[k, j : j + 1, :]
        out[ROWS + KN : ROWS + KN + 1, here] = act[:, j * LANES : (j + 1) * LANES].astype(jnp.float32)


def begin_kernel(out):
    out[...] = jnp.zeros(out.shape, out.dtype)


def begin():
    return pl.pallas_call(
        begin_kernel,
        out_shape=jax.ShapeDtypeStruct((8, LANES), jnp.float32),
        out_specs=VMEM,
        compiler_params=params(1),
        cost_estimate=pl.CostEstimate(flops=4_000_000_000, bytes_accessed=8_000_000, transcendentals=0),
        name="begin",
    )()


def pack_kernel(_, state, off, coef, act, near, chip):
    first = on_first_core()

    def both(run_end, high):
        for out, upper in ((chip, not high),) if run_end else ((chip, not high), (near, high)):
            start = COLS - EDGE if upper else 0
            out[0:ROWS, :] = state[:, start : start + EDGE]
            fill_lists(out, off, coef, act, upper)

    for run_end in (True, False):
        for low in (True, False):

            @pl.when(jnp.logical_and(at_run_end() == run_end, first == low))
            def _(run_end=run_end, low=low):
                both(run_end, not low)


def pack(state, off, coef, act):
    sent = jax.ShapeDtypeStruct((SENT, EDGE), jnp.float32)
    return pl.pallas_call(
        pack_kernel,
        out_shape=(sent, sent),
        in_specs=[VMEM] * 5,
        out_specs=(VMEM, VMEM),
        compiler_params=params(2),
        name="pack",
    )(begin(), state, off, coef, act)


def rim_kernel(near, out):
    first = on_first_core()
    for field in range(NF):
        row = slice(LEV * field, LEV * field + 1)
        out[field : field + 1, :] = jnp.where(first, near[row, HALO:EDGE], near[row, 0:HALO])


def rim(near):
    return pl.pallas_call(
        rim_kernel,
        out_shape=jax.ShapeDtypeStruct((NF, HALO), jnp.float32),
        in_specs=[VMEM],
        out_specs=VMEM,
        compiler_params=params(2),
        name="rim",
    )(near)


def widen_kernel(chip, edge, surf, out):
    first = on_first_core()
    out[:, HALO : HALO + COLS] = surf[...]
    for field in range(NF):
        row, this = slice(LEV * field, LEV * field + 1), slice(field, field + 1)
        out[this, 0:HALO] = jnp.where(first, edge[this, :], chip[row, HALO:EDGE])
        out[this, HALO + COLS :] = jnp.where(first, chip[row, 0:HALO], edge[this, :])


def widen(chip, edge, surf):
    return pl.pallas_call(
        widen_kernel,
        out_shape=jax.ShapeDtypeStruct((NF, MID), jnp.float32),
        in_specs=[VMEM, VMEM, VMEM],
        out_specs=VMEM,
        compiler_params=params(2),
        name="widen",
    )(chip, edge, surf)


def build_table(table, off, coef, first_panel):
    for part in range(BLOCK // LANES):
        at = pl.ds(first_panel + part, 1)
        lane = lax.broadcasted_iota(jnp.int32, (PANEL, LANES), 1)
        row = lax.broadcasted_iota(jnp.int32, (PANEL, LANES), 0)
        shift = lane - row + (HALO + part * LANES)
        offs = [jnp.broadcast_to(off[k, at, :], (PANEL, LANES)) for k in range(KN)]
        coefs = [jnp.broadcast_to(coef[k, at, :], (PANEL, LANES)) for k in range(KN)]
        high, low = [], []
        for k in range(KN):
            merged = coefs[k]
            for j in range(KN):
                if j != k:
                    merged = merged + jnp.where(offs[j] == offs[k], coefs[j], 0.0)
            top = merged.astype(jnp.bfloat16)
            high.append(top)
            low.append((merged - top.astype(jnp.float32)).astype(jnp.bfloat16))
        place = [(o + shift).astype(jnp.int16) for o in offs]
        none = jnp.zeros((PANEL, LANES), jnp.bfloat16)
        for start in range(0, WINDOW, PANEL):
            if start + PANEL <= part * LANES or start >= part * LANES + LANES + 2 * HALO:
                first, second = none, none
            else:
                first, second = none, none
                for k in range(KN):
                    hit = place[k] == jnp.int16(start)
                    first = jnp.where(hit, high[k], first)
                    second = jnp.where(hit, low[k], second)
            rows = slice(start, start + PANEL)
            table[rows, part * LANES : (part + 1) * LANES] = first
            table[rows, BLOCK + part * LANES : BLOCK + (part + 1) * LANES] = second


def split_into(parts, cols, value):
    top = value.astype(jnp.bfloat16)
    parts[0:ROWS, cols] = top
    parts[ROWS : 2 * ROWS, cols] = (value - top.astype(jnp.float32)).astype(jnp.bfloat16)


def relaxed(parts, table, start, centre, total, act):
    window = slice(start, start + WINDOW)
    both = jnp.dot(parts[:, window], table[:, 0:BLOCK], preferred_element_type=jnp.float32)
    rest = jnp.dot(parts[0:ROWS, window], table[:, BLOCK:], preferred_element_type=jnp.float32)
    gathered = both[0:ROWS] + both[ROWS:] + rest
    row = lax.broadcasted_iota(jnp.int32, (ROWS, BLOCK), 0)
    level = jnp.where(row >= LEV, row - LEV, row)
    return centre + jnp.where(level < act, gathered - total * centre, 0.0)


INSIDE = COLS - 2 * HALO
CORE = COLS - 2 * EDGE
OWN = COLS // BLOCK


def totals_of(totals, coef, start, count):
    for j in range(count):
        total = coef[0, j : j + 1, :]
        for k in range(1, KN):
            total = total + coef[k, j : j + 1, :]
        totals[:, start + j * LANES : start + (j + 1) * LANES] = total


def inner(state, off, coef, act, tables, mid, parts2, done, parts, totals):
    def table_of(b, carry):
        build_table(tables.at[b], off, coef, b * (BLOCK // LANES))
        return carry

    lax.fori_loop(0, OWN, table_of, 0)
    totals_of(totals, coef, 0, COLS // LANES)
    for b in range(OWN):
        cols = slice(b * BLOCK, (b + 1) * BLOCK)
        split_into(parts, cols, state[:, cols])
    for b in range(1, OWN - 1):
        cols = slice(b * BLOCK, (b + 1) * BLOCK)
        value = relaxed(parts, tables.at[b], (b - 1) * BLOCK, state[:, cols], totals[:, cols], act[:, cols])
        there = slice((b - 1) * BLOCK, b * BLOCK)
        mid[:, there] = value
        split_into(parts2, there, value)
    for b in range(2, OWN - 2):
        cols = slice(b * BLOCK, (b + 1) * BLOCK)
        centre = mid[:, (b - 1) * BLOCK : b * BLOCK]
        here = slice((b - 2) * BLOCK, (b - 1) * BLOCK)
        done[:, here] = relaxed(parts2, tables.at[b], (b - 2) * BLOCK, centre, totals[:, cols], act[:, cols])


INNER = (
    jax.ShapeDtypeStruct((OWN, WINDOW, 2 * BLOCK), jnp.bfloat16),
    jax.ShapeDtypeStruct((ROWS, INSIDE), jnp.float32),
    jax.ShapeDtypeStruct((2 * ROWS, INSIDE), jnp.bfloat16),
    jax.ShapeDtypeStruct((ROWS, CORE), jnp.float32),
)
INNER_SCRATCH = [pltpu.VMEM((2 * ROWS, COLS), jnp.bfloat16), pltpu.VMEM((1, COLS), jnp.float32)]


def inside_kernel(state, off, coef, act, tables, mid, parts2, done, surf, edge, far, parts, totals):
    first = on_first_core()
    for field in range(NF):
        row, this = slice(LEV * field, LEV * field + 1), slice(field, field + 1)
        surf[this, :] = state[row, :]
        edge[this, :] = jnp.where(first, state[row, 0:HALO], state[row, COLS - HALO :])

    for low in (True, False):

        @pl.when(jnp.logical_and(at_run_end(), first == low))
        def _(low=low):
            far[0:ROWS, :] = state[:, 0:EDGE] if low else state[:, COLS - EDGE :]
            fill_lists(far, off, coef, act, not low)

    @pl.when(goes_ahead())
    def _():
        inner(state, off, coef, act, tables, mid, parts2, done, parts, totals)


def inside(state, off, coef, act):
    return pl.pallas_call(
        inside_kernel,
        out_shape=INNER
        + (
            jax.ShapeDtypeStruct((NF, COLS), jnp.float32),
            jax.ShapeDtypeStruct((NF, HALO), jnp.float32),
            jax.ShapeDtypeStruct((SENT, EDGE), jnp.float32),
        ),
        in_specs=[VMEM, VMEM, VMEM, VMEM],
        out_specs=(VMEM,) * 7,
        scratch_shapes=INNER_SCRATCH,
        compiler_params=params(6),
        cost_estimate=pl.CostEstimate(flops=2_000_000_000, bytes_accessed=4_000_000, transcendentals=0),
        name="inside",
    )(state, off, coef, act)


def advance_kernel(
    state, chip, near, far, off, coef, act, tables_in, mid_in, parts_in, core_in, out, done, core_out,
    ends, mid_ends, parts, parts2, end_tables, end_off, end_coef, end_act, totals,
    tables_late, mid_late, parts_late, state_parts, state_totals, sem,
):
    first, run_end, ahead = on_first_core(), at_run_end(), goes_ahead()

    @pl.when(ahead)
    def _():
        core_out[...] = core_in[...]

    @pl.when(jnp.logical_not(ahead))
    def _():
        inner(state, off, coef, act, tables_late, mid_late, parts_late, core_out, state_parts, state_totals)

    write = pltpu.make_async_copy(core_out, out.at[:, pl.ds(EDGE, CORE)], sem)
    write.start()

    def received(side, rows, cols):
        other, mine = jnp.where(run_end, far[rows, cols], near[rows, cols]), chip[rows, cols]
        return jnp.where(first, other, mine) if side == 0 else jnp.where(first, mine, other)

    for side in range(2):
        for part in range(HALO // LANES):
            j = side * (HALO // LANES) + part
            here = slice(part * LANES, (part + 1) * LANES)
            there = slice(HALO + part * LANES, HALO + (part + 1) * LANES)
            lists = received(side, slice(ROWS, SENT), here)
            weights = received(side, slice(ROWS, SENT), there)
            for k in range(KN):
                end_off[k, j : j + 1, :] = lists[k : k + 1, :].astype(jnp.int32)
                end_coef[k, j : j + 1, :] = weights[k : k + 1, :]
            end_act[:, j * LANES : (j + 1) * LANES] = lists[KN : KN + 1, :].astype(jnp.int32)

    def table_of(b, carry):
        build_table(end_tables.at[b], end_off, end_coef, b * (BLOCK // LANES))
        return carry

    lax.fori_loop(0, 2, table_of, 0)
    totals_of(totals, coef, 0, COLS // LANES)
    totals_of(totals, end_coef, COLS, 2 * HALO // LANES)
    every = slice(0, ROWS)
    for side in range(2):
        for start in range(0, EDGE, BLOCK):
            cols = slice(start, start + BLOCK)
            value = received(side, every, cols)
            there = slice(start + side * EDGE, start + side * EDGE + BLOCK)
            ends[side, :, cols] = value
            split_into(parts.at[side], there, value)
            own = slice(start + side * (COLS - EDGE), start + side * (COLS - EDGE) + BLOCK)
            split_into(parts.at[side], slice(start + EDGE - side * EDGE, start + EDGE - side * EDGE + BLOCK), state[:, own])

    def end(side, block, table, centre, total, active):
        value = relaxed(parts.at[side], table, block * BLOCK, centre, total, active)
        mid_ends[side, :, block * BLOCK : (block + 1) * BLOCK] = value
        at = (side * OWN + block) * BLOCK
        split_into(parts2, slice(at, at + BLOCK), value)

    low, high = slice(0, BLOCK), slice(COLS - BLOCK, COLS)

    def finish(tables, mid, parts_mid):
        parts2[:, 2 * HALO : 2 * HALO + INSIDE] = parts_mid[...]
        for side, block in ((0, 0), (1, 1)):
            cols = slice(side * HALO, (side + 1) * HALO)
            centre = ends[side, :, HALO - side * HALO : EDGE - side * HALO]
            total = totals[:, COLS + side * HALO : COLS + (side + 1) * HALO]
            end(side, block, end_tables.at[side], centre, total, end_act[:, cols])
        end(0, 1, tables.at[0], state[:, low], totals[:, low], act[:, low])
        end(1, 0, tables.at[OWN - 1], state[:, high], totals[:, high], act[:, high])
        for at, b in enumerate((0, 1, OWN - 2, OWN - 1)):
            cols = slice(b * BLOCK, (b + 1) * BLOCK)
            if b == 0:
                centre = mid_ends[0, :, BLOCK : 2 * BLOCK]
            elif b == OWN - 1:
                centre = mid_ends[1, :, 0:BLOCK]
            else:
                centre = mid[:, (b - 1) * BLOCK : b * BLOCK]
            there = slice(at * BLOCK, (at + 1) * BLOCK)
            done[:, there] = relaxed(parts2, tables.at[b], b * BLOCK, centre, totals[:, cols], act[:, cols])

    @pl.when(ahead)
    def _():
        finish(tables_in, mid_in, parts_in)

    @pl.when(jnp.logical_not(ahead))
    def _():
        finish(tables_late, mid_late, parts_late)

    write.wait()


def advance(state, chip, near, far, off, coef, act, tables, mid, parts2, core):
    return pl.pallas_call(
        advance_kernel,
        out_shape=(
            jax.ShapeDtypeStruct((ROWS, COLS), jnp.float32),
            jax.ShapeDtypeStruct((ROWS, 2 * EDGE), jnp.float32),
            jax.ShapeDtypeStruct((ROWS, CORE), jnp.float32),
        ),
        in_specs=[VMEM] * 11,
        out_specs=(ANY, VMEM, VMEM),
        scratch_shapes=[
            pltpu.VMEM((2, ROWS, EDGE), jnp.float32),
            pltpu.VMEM((2, ROWS, EDGE), jnp.float32),
            pltpu.VMEM((2, 2 * ROWS, 2 * EDGE), jnp.bfloat16),
            pltpu.VMEM((2 * ROWS, MID), jnp.bfloat16),
            pltpu.VMEM((2, WINDOW, 2 * BLOCK), jnp.bfloat16),
            pltpu.VMEM((KN, 2 * HALO // LANES, LANES), jnp.int32),
            pltpu.VMEM((KN, 2 * HALO // LANES, LANES), jnp.float32),
            pltpu.VMEM((1, 2 * HALO), jnp.int32),
            pltpu.VMEM((1, MID), jnp.float32),
        ]
        + [pltpu.VMEM(kept.shape, kept.dtype) for kept in INNER[:3]]
        + INNER_SCRATCH
        + [pltpu.SemaphoreType.DMA],
        compiler_params=params(24),
        cost_estimate=pl.CostEstimate(flops=6_000_000_000, bytes_accessed=4_000_000, transcendentals=0),
        name="advance",
    )(state, chip, near, far, off, coef, act, tables, mid, parts2, core)


def couple_kernel(got, beyond, ioff, iweight, act, relax, core, ends, _, remapped, out, partner, tiles, found_all, sems):
    writes = []
    for side in range(2):
        for field in range(NF):
            rows = pl.ds(LEV * field + 8, LEV - 8)
            writes.append(
                pltpu.make_async_copy(
                    ends.at[rows, pl.ds(side * EDGE, EDGE)],
                    out.at[rows, pl.ds(side * (COLS - EDGE), EDGE)],
                    sems.at[NF * side + field],
                )
            )
    for copy in writes:
        copy.start()
    first, run_end = on_first_core(), at_run_end()
    left, right = slice(0, HALO), slice(HALO + COLS, MID)
    partner[:, HALO : HALO + COLS] = got[:, HALO : HALO + COLS]
    partner[:, left] = jnp.where(jnp.logical_and(run_end, first), beyond[...], got[:, left])
    partner[:, right] = jnp.where(jnp.logical_and(run_end, jnp.logical_not(first)), beyond[...], got[:, right])
    lane = lax.broadcasted_iota(jnp.int32, (KR, LANES), 1)
    for b in range(COLS // LANES):
        cols = slice(b * LANES, (b + 1) * LANES)
        place = ioff[:, cols] + lane + HALO
        chunk = lax.shift_right_logical(place, 7)
        at = jnp.bitwise_and(place, LANES - 1)
        weights = iweight[:, cols]
        for field in range(NF):
            nearby = jnp.zeros((KR, LANES), jnp.float32)
            for q in range(1 + 2 * HALO // LANES):
                source = jnp.broadcast_to(
                    partner[field : field + 1, (b + q) * LANES : (b + q + 1) * LANES], (KR, LANES)
                )
                found = jnp.take_along_axis(source, at, axis=1, mode="promise_in_bounds")
                nearby = jnp.where(chunk == q, found, nearby)
            found_all[field : field + 1, cols] = jnp.sum(weights * nearby, axis=0, keepdims=True)
    copy = pltpu.make_async_copy(found_all, remapped, sems.at[2 * NF])
    copy.start()
    writes.append(copy)
    for field in range(NF):
        rows = slice(LEV * field, LEV * field + 8)
        tiles[field, :, 0:EDGE] = ends[rows, 0:EDGE]
        tiles[field, :, EDGE : EDGE + CORE] = core[rows, :]
        tiles[field, :, EDGE + CORE :] = ends[rows, EDGE:]
        before, value = tiles[field, 0:1, :], found_all[field : field + 1, :]
        tiles[field, 0:1, :] = before + jnp.where(act[...] > 0, relax[0:1, field : field + 1] * (value - before), 0.0)
        copy = pltpu.make_async_copy(
            tiles.at[field], out.at[pl.ds(LEV * field, 8), :], sems.at[2 * NF + 1 + field]
        )
        copy.start()
        writes.append(copy)
    for copy in writes:
        copy.wait()


def couple(partner, beyond, ioff, iweight, act, relax, core, ends, out):
    return pl.pallas_call(
        couple_kernel,
        out_shape=(
            jax.ShapeDtypeStruct((NF, COLS), jnp.float32),
            jax.ShapeDtypeStruct((ROWS, COLS), jnp.float32),
        ),
        in_specs=[VMEM, VMEM, VMEM, VMEM, VMEM, VMEM, VMEM, VMEM, ANY],
        out_specs=(ANY, ANY),
        scratch_shapes=[
            pltpu.VMEM((NF, MID), jnp.float32),
            pltpu.VMEM((NF, 8, COLS), jnp.float32),
            pltpu.VMEM((NF, COLS), jnp.float32),
            pltpu.SemaphoreType.DMA((3 * NF + 1,)),
        ],
        input_output_aliases={8: 1},
        compiler_params=params(4),
        name="couple",
    )(partner, beyond, ioff, iweight, act, relax, core, ends, out)


def body(
    column_state,
    neighbour_offsets,
    edge_coefficients,
    active_levels,
    intersection_offsets,
    intersection_weights,
    relaxation,
):
    count = lax.axis_size("col")
    same_chip = [(i, i ^ 1) for i in range(count)]
    pairs = [p for i in range(1, count - 1, 2) for p in ((i, i + 1), (i + 1, i))]
    long = [(i, j) for i, j in pairs if i // RUN != j // RUN]
    short = [(i, j) for i, j in pairs if i // RUN == j // RUN]
    across = [(c * count + i, (1 - c) * count + j) for c in range(2) for i, j in long]
    state = column_state.reshape(ROWS, COLS)
    off = neighbour_offsets.reshape(KN, COLS // LANES, LANES)
    coef = edge_coefficients.reshape(KN, COLS // LANES, LANES)
    near, chip = pack(state, off, coef, active_levels)
    chip = lax.ppermute(chip, "col", same_chip)
    near = lax.ppermute(near, "col", short)
    tables, mid, parts, core, surface, edge, far = inside(state, off, coef, active_levels)
    far = lax.ppermute(far, "col", long)
    beyond = lax.ppermute(edge, ("comp", "col"), across)
    partner = lax.ppermute(widen(chip, rim(near), surface), "comp", [(0, 1), (1, 0)])
    out, ends, core = advance(state, chip, near, far, off, coef, active_levels, tables, mid, parts, core)
    remapped, coupled = couple(
        partner, beyond, intersection_offsets[0], intersection_weights[0], active_levels, relaxation, core, ends, out
    )
    return (coupled.reshape(1, NF, LEV, COLS), remapped.reshape(1, NF, COLS))


def solution(mesh):
    return jax.shard_map(
        body,
        mesh=mesh,
        in_specs=(
            P("comp", None, None, "col"),
            P("comp", None, "col"),
            P("comp", None, "col"),
            P("comp", "col"),
            P("comp", None, "col"),
            P("comp", None, "col"),
            P("comp", None),
        ),
        out_specs=(P("comp", None, None, "col"), P("comp", None, "col")),
        check_vma=False,
    )
```
